128 devices in a mesh: az: 16 (over z_lo, x, core), wn: 8 (over y, z_hi).
Axes of the slice: x: 4, y: 4, z: 4 (z_hi: 2, z_lo: 2; z = z_hi * 2 + z_lo), core: 2. Of those that a mesh axis runs over, the one named last changes fastest.
Arguments:
- state: float32 [5, 32, 96, 2048], P(None, 'wn', None, 'az'), may hold values from -6 to 6
- base_flow: float32 [2, 32, 96], P(None, 'wn'), may hold values from -1 to 1
- az_scale: float32 [96], replicated, may hold values from 1 to 5
- blow_table: float32 [16], replicated, may hold values from 0.5 to 2
- seg_index: int32 [96, 2048], P(None, 'az'), may hold values from 0 to 15
- porous: int32 [96, 2048], P(None, 'az'), may hold values 0 or 1
Outputs:
- final_state: float32 [5, 32, 96, 2048], P(None, 'wn', None, 'az')
The draws below stay inside these ranges and needn't reach their ends.
All inputs are finite; a program needn't handle non-finite values. No bound on the sum of `porous` on one device may be relied on, other than what follows from the above.
Results may differ from the reference program's by a relative error of at most 0.00002.
Values sent between devices are 32-bit elements; how exact they have to be, the bound alone decides.
No kernel may reach another device: no remote copies, remote signals or barrier semaphores. Data moves between devices by JAX's collectives and lax.ppermute only.
A program may use at most 128 MiB of HBM per device.

```python
import math
import jax
import jax.numpy as jnp

NP = 96
NSEG = 16
STEPS = 3
NA = 2048
NR = 32


def touch_ends(result, stream_key, least, largest):
    place = [jax.random.randint(jax.random.fold_in(stream_key, axis), (), 0, length) for axis, length in enumerate(result.shape)]
    main_axis = result.shape.index(max(result.shape))
    neighbour = place[:main_axis] + [(place[main_axis] + 1) % result.shape[main_axis]] + place[main_axis + 1:]
    return result.at[tuple(place)].set(least).at[tuple(neighbour)].set(largest)


def level_of(stream_key, shape, pieces, least, high):
    def one(dim, blocks):
        draws = jax.random.uniform(jax.random.fold_in(jax.random.fold_in(stream_key, 6), dim), (blocks,), jnp.float32, least / len(pieces), high / len(pieces))
        return jnp.repeat(jnp.exp(draws), shape[dim] // blocks).reshape((-1,) + (1,) * (len(shape) - dim - 1))

    gain = one(*pieces[0])
    for cut in pieces[1:]:
        gain = gain * one(*cut)
    return gain


def normal_values(rng, dims, deviation, bound, shards=(), kind=jnp.bfloat16):
    factor_of = level_of(rng, dims, shards, -0.22, 0.18) if shards else 1.0
    values = jax.random.normal(rng, dims, jnp.float32) * deviation * factor_of
    return jnp.minimum(jnp.maximum(values, -bound), bound).astype(kind)


def setup_inputs(seed: int = 0) -> dict:
    key_list = jax.random.split(jax.random.key(seed), 7)
    state = normal_values(key_list[0], (5, NR, NP, NA), 1.0, 6.0, ((1, 8), (3, 16)), jnp.float32)
    base_flow = jnp.clip(jax.random.uniform(key_list[1], (2, NR, NP), jnp.float32, -1.0, 1.0) * level_of(key_list[1], (2, NR, NP), ((1, 8),), -0.4, 0.0), -1.0, 1.0)
    az_scale = jnp.clip(jnp.exp(jax.random.uniform(key_list[2], (NP,), jnp.float32, math.log(1.0), math.log(5.0))), 1.0, 5.0)
    blow_table = jnp.clip(jnp.exp(jax.random.uniform(key_list[3], (NSEG,), jnp.float32, math.log(0.5), math.log(2.0))), 0.5, 2.0)
    seg_index = touch_ends(jax.random.randint(key_list[4], (NP, NA), 0, NSEG), jax.random.fold_in(key_list[4], 1), 0, NSEG - 1).astype(jnp.int32)
    porous = touch_ends((jax.random.randint(key_list[5], (NP, NA), 0, 3) < 1).astype(jnp.int32), jax.random.fold_in(key_list[5], 1), 0, 1)
    return dict(state=state, base_flow=base_flow, az_scale=az_scale, blow_table=blow_table, seg_index=seg_index, porous=porous)


time_step = 0.25
viscosity = 0.05
heat_ratio = 1.4
admittance = 0.6


def wall_ghost(first_layer, blowing, porous):
    radial = jnp.where(porous == 1, 2.0 * admittance * first_layer[4] - first_layer[1], 2.0 * blowing - first_layer[1])
    return jnp.stack([first_layer[0], radial, -first_layer[2], -first_layer[3], first_layer[4]])


def pole_ghost(partner):
    signs = jnp.array([1.0, 1.0, -1.0, -1.0, 1.0], jnp.float32).reshape(5, 1, 1)
    return signs * partner


def tendency(state, padded_r, padded_t, grad_a, vel_slopes, base_flow, az_scale):
    grad_r = (padded_r[:, 2:] - padded_r[:, :-2]) * 0.5
    curv_r = padded_r[:, 2:] - 2.0 * state + padded_r[:, :-2]
    grad_t = (padded_t[:, :, 2:] - padded_t[:, :, :-2]) * 0.5
    curv_t = padded_t[:, :, 2:] - 2.0 * state + padded_t[:, :, :-2]
    curv_a = (vel_slopes[..., 2:] - vel_slopes[..., :-2]) * 0.5
    radial_speed = base_flow[0][:, :, None]
    polar_speed = base_flow[1][:, :, None]
    metric = az_scale[None, :, None]
    advect = radial_speed * grad_r + polar_speed * grad_t
    diverge = grad_r[1] + grad_t[2] + metric * grad_a[3]
    diffuse = viscosity * (curv_r[1:4] + curv_t[1:4] + metric * metric * curv_a)
    return jnp.stack([
        -advect[0] - diverge,
        -advect[1] - grad_r[4] + diffuse[0],
        -advect[2] - grad_t[4] + diffuse[1],
        -advect[3] - metric * grad_a[4] + diffuse[2],
        -advect[4] - heat_ratio * diverge])


def forcing(state, base_flow, az_scale, blowing, porous):
    lower = wall_ghost(state[:, 0], blowing, porous)
    padded_r = jnp.concatenate([lower[:, None], state, jnp.zeros_like(state[:, :1])], 1)
    half_turn = state.shape[3] // 2
    partner = jnp.roll(state[:, :, 0, :], -half_turn, axis=-1)
    padded_t = jnp.concatenate([pole_ghost(partner)[:, :, None], state, jnp.zeros_like(state[:, :, :1])], 2)
    padded_a = jnp.concatenate([state[..., -2:], state, state[..., :2]], 3)
    slopes = (padded_a[..., 2:] - padded_a[..., :-2]) * 0.5
    return tendency(state, padded_r, padded_t, slopes[..., 1:-1], slopes[1:4], base_flow, az_scale)


def reference(state, base_flow, az_scale, blow_table, seg_index, porous):
    segments = jnp.arange(blow_table.shape[0], dtype=jnp.int32)
    blowing = jnp.sum(jnp.where(seg_index[..., None] == segments, blow_table, jnp.float32(0.0)), -1)
    current = state
    for step_index in range(STEPS):
        slope_one = forcing(current, base_flow, az_scale, blowing, porous)
        slope_two = forcing(current + 0.125 * slope_one, base_flow, az_scale, blowing, porous)
        slope_three = forcing(current + 0.125 * slope_two, base_flow, az_scale, blowing, porous)
        slope_four = forcing(current + 0.25 * slope_three, base_flow, az_scale, blowing, porous)
        current = current + (time_step / 6.0) * (slope_one + 2.0 * slope_two + 2.0 * slope_three + slope_four)
    return current
```

```python
import jax
import jax.numpy as jnp
from jax import lax
from jax.experimental import pallas as pl
from jax.experimental.pallas import tpu as pltpu
from jax.sharding import PartitionSpec as P

STEPS = 3
time_step = 0.25
viscosity = 0.05
heat_ratio = 1.4
admittance = 0.6

REACH = 12
OWN_T = 24
ROWS = OWN_T + 2 * REACH
SIDE = 32
SIGNS = (1.0, 1.0, -1.0, -1.0, 1.0)
VMEM = pl.BlockSpec(memory_space=pltpu.VMEM)
SMEM = pl.BlockSpec(memory_space=pltpu.SMEM)


def lane_of(shape):
    return lax.broadcasted_iota(jnp.int32, shape, len(shape) - 1)


def roll(x, shift):
    shift = shift % 128
    return pltpu.roll(x, shift, x.ndim - 1) if shift else x


def edges_kernel(table, state, seg, porous, walls, head, tail):
    seg_now = seg[...]
    blowing = jnp.zeros(seg_now.shape, jnp.float32)
    for k in range(16):
        blowing = jnp.where(seg_now == k, table[k], blowing)
    walls[0] = 2.0 * blowing
    walls[1] = porous[...].astype(jnp.float32)
    group = lane_of((96, 128)) // SIDE

    def pack(parts, start):
        out = jnp.zeros((96, 128), jnp.float32)
        for i, part in enumerate(parts):
            out = jnp.where(group == i, roll(part, SIDE * i - start), out)
        return out

    for c in range(5):
        parts = [state[c * 4 + l] for l in range(4)]
        head[c] = pack(parts, 0)
        tail[c] = pack(parts, 128 - SIDE)
    parts = [walls[0], walls[1]]
    head[5] = pack(parts, 0)
    tail[5] = pack(parts, 128 - SIDE)


def windows_kernel(place, state, walls, flow, before, after, pole, pieces, wall_window):
    quarter, half = place[0], place[1]

    def window(own, left, right, group):
        lane = lane_of(own.shape)
        first = jnp.where(lane < SIDE, roll(left, -SIDE * group), roll(own, SIDE))
        second = jnp.where(
            lane >= 128 - SIDE, roll(right, 128 - SIDE - SIDE * group), roll(own, -SIDE)
        )
        return first, second

    for c in range(5):
        for l in range(4):
            ch = c * 4 + l
            mine = window(state[ch], before[c], after[c], l)
            ghost = window(pole[ch], pole[22 + c], pole[28 + c], l)
            for h in range(2):
                pieces[h, ch, 0:12] = SIGNS[c] * ghost[h]
                pieces[h, ch, 12:48] = mine[h][0:36]
                pieces[2 + h, ch] = mine[h][12:60]
                pieces[4 + h, ch] = mine[h][36:84]
                pieces[6 + h, ch, 0:36] = mine[h][60:96]
                pieces[6 + h, ch, 36:48] = jnp.zeros((12, 128), jnp.float32)
    lane = lane_of((ROWS, 128))
    for l in range(4):
        for q in range(4):
            layer = flow[l, OWN_T * q : OWN_T * q + ROWS]
            for h in range(2):
                pieces[2 * q + h, l] = jnp.where(lane < 2, layer, pieces[2 * q + h, l])
    for k in range(2):
        mine = window(walls[k], before[5], after[5], k)
        ghost = window(pole[20 + k], pole[27], pole[33], k)
        mine = jnp.where(half == 0, mine[0], mine[1])
        ghost = jnp.where(half == 0, ghost[0], ghost[1])
        zeros = jnp.zeros((12, 128), jnp.float32)
        wall_window[k] = jnp.where(
            quarter == 0,
            jnp.concatenate([ghost, mine[0:36]], 0),
            jnp.where(
                quarter == 1,
                mine[12:60],
                jnp.where(quarter == 2, mine[36:84], jnp.concatenate([mine[60:96], zeros], 0)),
            ),
        )


def steps_kernel(start, metric, valid, wall, out, speed, buf_b, buf_c, buf_d):
    nu = viscosity
    lane = lane_of((8, 128))

    def spread(w, _):
        for l in range(4):
            layer = 0.5 * start[w * 20 + l]
            for k in range(2):
                speed[k, w * 4 + l] = jnp.broadcast_to(layer[:, k : k + 1], (ROWS, 128))
        return 0

    lax.fori_loop(0, 8, spread, 0)

    def stage_pass(source, base, target, scale, stage, last):
        low, high = stage, ROWS - stage

        def chunk(i, _):
            t0 = jnp.minimum(low + 8 * i, high - 8)
            here = pl.ds(t0, 8)
            m = metric[here, :]
            cm = scale * valid[here, :]
            ch = 0.5 * cm
            c_nu = nu * cm
            ca = (0.25 * c_nu) * (m * m)
            cc = -(4.0 * c_nu + 2.0 * ca)
            cmm = ch * m
            blow = wall[0, here, :]
            coated = wall[1, here, :] > 0.5

            def read(ref, w, c, l, rows=here):
                return ref[w * 20 + c * 4 + l, rows, :]

            def advance(w, carry):
                before, now = carry
                saved = []
                for l in range(4):
                    r = w * 4 + l + 1
                    if r < 32:
                        after = [read(source, r // 4, c, r % 4) for c in range(5)]
                    else:
                        after = [jnp.zeros((8, 128), jnp.float32)] * 5
                    down = [read(source, w, c, l, pl.ds(t0 - 1, 8)) for c in range(5)]
                    up = [read(source, w, c, l, pl.ds(t0 + 1, 8)) for c in range(5)]
                    hu = cm * speed[0, w * 4 + l, here, :]
                    hv = cm * speed[1, w * 4 + l, here, :]
                    rp, rm, tp, tm = c_nu - hu, c_nu + hu, c_nu - hv, c_nu + hv
                    dr_p = after[4] - before[4]
                    dt_p = up[4] - down[4]
                    da_p = roll(now[4], -1) - roll(now[4], 1)
                    div = (after[1] - before[1]) + (up[2] - down[2])
                    div = div + m * (roll(now[3], -1) - roll(now[3], 1))
                    div = ch * div
                    adv = hu * (after[0] - before[0]) + hv * (up[0] - down[0])
                    adv_p = hu * dr_p + hv * dt_p
                    old = [read(base, w, c, l) for c in range(5)]
                    new = [old[0] - adv - div, None, None, None, old[4] - adv_p - heat_ratio * div]
                    push = [None, ch * dr_p, ch * dt_p, cmm * da_p]
                    for c in (1, 2, 3):
                        v = rp * after[c] + rm * before[c] + tp * up[c] + tm * down[c]
                        v = v + ca * (roll(now[c], 2) + roll(now[c], -2)) + cc * now[c]
                        new[c] = old[c] + (v - push[c])
                    if not last:
                        for c in range(5):
                            target[w * 20 + c * 4 + l, here, :] = new[c]
                    elif l % 2 == 0:
                        saved = new
                    else:
                        for c in range(5):
                            both = jnp.where(
                                lane < 64, roll(saved[c], -SIDE), roll(new[c], 64 - SIDE)
                            )
                            out[w, c * 2 + l // 2, pl.ds(t0 - REACH, 8), :] = both
                    before, now = now, after
                return before, now

            first = [read(source, 0, c, 0) for c in range(5)]
            ghost_u = jnp.where(coated, (2.0 * admittance) * first[4], blow) - first[1]
            ghost = [first[0], ghost_u, -first[2], -first[3], first[4]]
            carry = (ghost, first)
            for w in range(8):
                carry = advance(w, carry)
            return 0

        lax.fori_loop(0, (high - low + 7) // 8, chunk, 0)

    h = time_step
    bases = [start, buf_d, start]
    stage = 0
    for step in range(STEPS):
        base = start if step == 0 else buf_d
        plan = [
            (base, buf_b, h / 4.0),
            (buf_b, buf_c, h / 3.0),
            (buf_c, buf_b, h / 2.0),
            (buf_b, buf_d, h),
        ]
        if step == 1:
            plan[3] = (buf_b, buf_c, h)
        if step == 2:
            base = buf_c
            plan = [
                (buf_c, buf_b, h / 4.0),
                (buf_b, buf_d, h / 3.0),
                (buf_d, buf_b, h / 2.0),
                (buf_b, None, h),
            ]
        for source, target, scale in plan:
            stage += 1
            stage_pass(source, base, target, scale, stage, stage == 4 * STEPS)


def unpack_kernel(got, out):
    lane = lane_of((24, 128))
    for q in range(4):
        rows = pl.ds(24 * q, 24)
        for c in range(5):
            for pair in range(2):
                a = got[2 * q, c * 2 + pair]
                b = got[2 * q + 1, c * 2 + pair]
                out[c, 2 * pair, rows, :] = jnp.where(lane < 64, a, roll(b, 64))
                out[c, 2 * pair + 1, rows, :] = jnp.where(lane < 64, roll(a, 64), b)


def shape(*dims):
    return jax.ShapeDtypeStruct(dims, jnp.float32)


def params(mib):
    return pltpu.CompilerParams(vmem_limit_bytes=mib << 20)


def local(state, base_flow, az_scale, blow_table, seg_index, porous):
    place = lax.axis_index("wn")
    quarter, half = place // 2, place % 2
    cells = state.reshape(20, 96, 128)
    walls, head, tail = pl.pallas_call(
        edges_kernel,
        out_shape=(shape(2, 96, 128), shape(6, 96, 128), shape(6, 96, 128)),
        in_specs=[SMEM, VMEM, VMEM, VMEM],
        out_specs=(VMEM, VMEM, VMEM),
        compiler_params=params(24),
        name="edges",
    )(blow_table, cells, seg_index, porous)
    count = lax.axis_size("az")
    before = lax.ppermute(tail, "az", [(i, (i + 1) % count) for i in range(count)])
    after = lax.ppermute(head, "az", [((i + 1) % count, i) for i in range(count)])
    near = jnp.concatenate(
        [cells[:, :REACH], walls[:, :REACH], before[:, :REACH], after[:, :REACH]], 0
    )
    pole = lax.ppermute(
        jnp.flip(near, 1), "az", [(i, (i + count // 2) % count) for i in range(count)]
    )
    def cycles(x, sign):
        return jnp.concatenate(
            [sign * x[..., REACH - 1 :: -1], x, jnp.zeros_like(x[..., :REACH])], -1
        )

    flow = jnp.stack([cycles(base_flow[0], 1.0), cycles(base_flow[1], -1.0)], -1)
    flow = jnp.pad(flow, ((0, 0), (0, 0), (0, 126)))
    pieces, wall_window = pl.pallas_call(
        windows_kernel,
        out_shape=(shape(8, 20, ROWS, 128), shape(2, ROWS, 128)),
        in_specs=[SMEM] + [VMEM] * 6,
        out_specs=(VMEM, VMEM),
        compiler_params=params(32),
        name="windows",
    )(jnp.stack([quarter, half]).astype(jnp.int32), cells, walls, flow, before, after, pole)

    near_axis = lax.dynamic_slice_in_dim(cycles(az_scale, -1.0), OWN_T * quarter, ROWS)
    metric = jnp.broadcast_to(near_axis[:, None], (ROWS, 128))
    cycle = lax.broadcasted_iota(jnp.int32, (ROWS, 128), 0) + (OWN_T * quarter - REACH)
    valid = jnp.where(cycle < 96, 1.0, 0.0).astype(jnp.float32)

    got = lax.all_to_all(pieces, "wn", 0, 0, tiled=True)
    done = pl.pallas_call(
        steps_kernel,
        out_shape=shape(8, 10, OWN_T, 128),
        in_specs=[VMEM] * 4,
        out_specs=VMEM,
        scratch_shapes=[pltpu.VMEM((2, 32, ROWS, 128), jnp.float32)]
        + [pltpu.VMEM((160, ROWS, 128), jnp.float32)] * 3,
        compiler_params=params(48),
        name="steps",
    )(got.reshape(160, ROWS, 128), metric, valid, wall_window)
    back = lax.all_to_all(done, "wn", 0, 0, tiled=True)
    return pl.pallas_call(
        unpack_kernel,
        out_shape=shape(5, 4, 96, 128),
        in_specs=[VMEM],
        out_specs=VMEM,
        compiler_params=params(24),
        name="unpack",
    )(back)


def solution(mesh):
    return jax.shard_map(
        local,
        mesh=mesh,
        in_specs=(
            P(None, "wn", None, "az"),
            P(None, "wn", None),
            P(),
            P(),
            P(None, "az"),
            P(None, "az"),
        ),
        out_specs=P(None, "wn", None, "az"),
        check_vma=False,
    )
```

```python
import jax
import jax.numpy as jnp
from jax import lax
from jax.experimental import pallas as pl
from jax.experimental.pallas import tpu as pltpu
from jax.sharding import PartitionSpec as P

STEPS = 3
time_step = 0.25
viscosity = 0.05
heat_ratio = 1.4
admittance = 0.6

REACH = 12
OWN_T = 24
ROWS = OWN_T + 2 * REACH
SIDE = 32
FLOW = 10 * ROWS
SIGNS = (1.0, 1.0, -1.0, -1.0, 1.0)
VMEM = pl.BlockSpec(memory_space=pltpu.VMEM)
SMEM = pl.BlockSpec(memory_space=pltpu.SMEM)


def lane_of(shape):
    return lax.broadcasted_iota(jnp.int32, shape, len(shape) - 1)


def roll(x, shift):
    shift = shift % 128
    return pltpu.roll(x, shift, x.ndim - 1) if shift else x


def low_lanes(shape):
    return lane_of(shape) < 64


def inner_lanes(shape):
    return lane_of(shape) % 64 < SIDE


def halves_kernel(core, table, state, seg, porous, keep, send, keep_pole, send_pole):
    first = core[0] == 0
    low = low_lanes((96, 128))

    def split(tile, even, odd, sign):
        left = jnp.where(low, even, roll(odd, 64))
        right = jnp.where(low, roll(even, 64), odd)
        keep[tile] = jnp.where(first, left, right)
        send[tile] = jnp.where(first, right, left)
        for i in range(REACH):
            keep_pole[tile, pl.ds(REACH - 1 - i, 1), :] = sign * keep[tile, pl.ds(i, 1), :]
            send_pole[tile, pl.ds(REACH - 1 - i, 1), :] = sign * send[tile, pl.ds(i, 1), :]

    for c in range(5):
        for i in range(2):
            split(c * 2 + i, state[c * 4 + 2 * i], state[c * 4 + 2 * i + 1], SIGNS[c])
    seg_now = seg[...]
    blowing = jnp.zeros(seg_now.shape, jnp.float32)
    for k in range(16):
        blowing = jnp.where(seg_now == k, table[k], blowing)
    split(10, 2.0 * blowing, porous[...].astype(jnp.float32), 1.0)


def windows_kernel(place, keep, got, keep_pole, got_pole, flow, pieces, wall):
    quarter, deep, flip = place[0], place[1], place[2]

    def window(block, pole, tile, q):
        if q == 0:
            return jnp.concatenate([pole[tile], block[tile, 0:36, :]], 0)
        if q == 3:
            return jnp.concatenate([block[tile, 60:96, :], jnp.zeros((12, 128), jnp.float32)], 0)
        return block[tile, 24 * q - 12 : 24 * q + 36, :]

    for block, pole, spot in ((keep, keep_pole, flip), (got, got_pole, 1 - flip)):
        for q in range(4):
            for tile in range(10):
                pieces[2 * q + spot, tile * ROWS : (tile + 1) * ROWS, :] = window(
                    block, pole, tile, q
                )
            pieces[2 * q + spot, FLOW : FLOW + 8, :] = flow[q]

            @pl.when(jnp.logical_and(quarter == q, deep == spot))
            def _():
                wall[...] = window(block, pole, 10, q)


def edges_kernel(got, wall, head, tail):
    inner = inner_lanes((ROWS, 128))

    def pack(w, _):
        for c in range(5):
            one = got[w, 2 * c * ROWS : (2 * c + 1) * ROWS, :]
            two = got[w, (2 * c + 1) * ROWS : (2 * c + 2) * ROWS, :]
            turned = roll(one, 64)
            head[w * 5 + c] = jnp.where(inner, turned, roll(two, 64 + SIDE))
            tail[w * 5 + c] = jnp.where(inner, roll(two, 64 - SIDE), turned)
        return 0

    lax.fori_loop(0, 8, pack, 0)
    turned = roll(wall[...], 64)
    head[40] = turned
    tail[40] = turned


def steps_kernel(
    got, head, tail, speed, metric, valid, packed_wall, out, start, wall, buf_b, buf_c, buf_d
):
    nu = viscosity
    lane = lane_of((8, 128))

    low = low_lanes((ROWS, 128))
    inner = inner_lanes((ROWS, 128))

    def widen(own, sides):
        return jnp.where(low, own, sides), roll(jnp.where(low, sides, own), 64)

    def spread(w, _):
        for c in range(5):
            right, left = head[w * 5 + c], tail[w * 5 + c]
            one = got[w, 2 * c * ROWS : (2 * c + 1) * ROWS, :]
            two = got[w, (2 * c + 1) * ROWS : (2 * c + 2) * ROWS, :]
            pair = widen(one, jnp.where(inner, right, left))
            pair += widen(two, jnp.where(inner, roll(right, -SIDE), roll(left, SIDE)))
            for l in range(4):
                start[w * 20 + c * 4 + l] = pair[l]
        return 0

    lax.fori_loop(0, 8, spread, 0)
    wall[0], wall[1] = widen(packed_wall[...], jnp.where(inner, head[40], tail[40]))

    def stage_pass(source, base, target, scale, stage, last):
        low, high = stage, ROWS - stage

        def chunk(i, _):
            t0 = jnp.minimum(low + 8 * i, high - 8)
            here = pl.ds(t0, 8)
            m = metric[here, :]
            cm = scale * valid[here, :]
            ch = 0.5 * cm
            c_nu = nu * cm
            ca = (0.25 * c_nu) * (m * m)
            cc = -(4.0 * c_nu + 2.0 * ca)
            cmm = ch * m
            blow = wall[0, here, :]
            coated = wall[1, here, :] > 0.5

            def read(ref, w, c, l, rows=here):
                return ref[w * 20 + c * 4 + l, rows, :]

            def advance(w, carry):
                before, now = carry
                saved = []
                for l in range(4):
                    r = w * 4 + l + 1
                    if r < 32:
                        after = [read(source, r // 4, c, r % 4) for c in range(5)]
                    else:
                        after = [jnp.zeros((8, 128), jnp.float32)] * 5
                    down = [read(source, w, c, l, pl.ds(t0 - 1, 8)) for c in range(5)]
                    up = [read(source, w, c, l, pl.ds(t0 + 1, 8)) for c in range(5)]
                    hu = cm * speed[0, w * 4 + l, here, :]
                    hv = cm * speed[1, w * 4 + l, here, :]
                    rp, rm, tp, tm = c_nu - hu, c_nu + hu, c_nu - hv, c_nu + hv
                    dr_p = after[4] - before[4]
                    dt_p = up[4] - down[4]
                    da_p = roll(now[4], -1) - roll(now[4], 1)
                    div = (after[1] - before[1]) + (up[2] - down[2])
                    div = div + m * (roll(now[3], -1) - roll(now[3], 1))
                    div = ch * div
                    adv = hu * (after[0] - before[0]) + hv * (up[0] - down[0])
                    adv_p = hu * dr_p + hv * dt_p
                    old = [read(base, w, c, l) for c in range(5)]
                    new = [old[0] - adv - div, None, None, None, old[4] - adv_p - heat_ratio * div]
                    push = [None, ch * dr_p, ch * dt_p, cmm * da_p]
                    for c in (1, 2, 3):
                        v = rp * after[c] + rm * before[c] + tp * up[c] + tm * down[c]
                        v = v + ca * (roll(now[c], 2) + roll(now[c], -2)) + cc * now[c]
                        new[c] = old[c] + (v - push[c])
                    if not last:
                        for c in range(5):
                            target[w * 20 + c * 4 + l, here, :] = new[c]
                    elif l % 2 == 0:
                        saved = new
                    else:
                        for c in range(5):
                            both = jnp.where(
                                lane < 64, saved[c], roll(new[c], 64)
                            )
                            out[w, c * 2 + l // 2, pl.ds(t0 - REACH, 8), :] = both
                    before, now = now, after
                return before, now

            first = [read(source, 0, c, 0) for c in range(5)]
            ghost_u = jnp.where(coated, (2.0 * admittance) * first[4], blow) - first[1]
            ghost = [first[0], ghost_u, -first[2], -first[3], first[4]]
            carry = (ghost, first)
            for w in range(8):
                carry = advance(w, carry)
            return 0

        lax.fori_loop(0, (high - low + 7) // 8, chunk, 0)

    h = time_step
    bases = [start, buf_d, start]
    stage = 0
    for step in range(STEPS):
        base = start if step == 0 else buf_d
        plan = [
            (base, buf_b, h / 4.0),
            (buf_b, buf_c, h / 3.0),
            (buf_c, buf_b, h / 2.0),
            (buf_b, buf_d, h),
        ]
        if step == 1:
            plan[3] = (buf_b, buf_c, h)
        if step == 2:
            base = buf_c
            plan = [
                (buf_c, buf_b, h / 4.0),
                (buf_b, buf_d, h / 3.0),
                (buf_d, buf_b, h / 2.0),
                (buf_b, None, h),
            ]
        for source, target, scale in plan:
            stage += 1
            stage_pass(source, base, target, scale, stage, stage == 4 * STEPS)


def join_kernel(place, back, got, out):
    flip, first = place[0], place[1] == 0
    low = low_lanes((OWN_T, 128))
    for q in range(4):
        rows = pl.ds(OWN_T * q, OWN_T)
        for c in range(5):
            for i in range(2):
                mine, other = back[2 * q + flip, c * 2 + i], got[q, c * 2 + i]
                left = jnp.where(first, mine, other)
                right = jnp.where(first, other, mine)
                out[c, 2 * i, rows, :] = jnp.where(low, left, roll(right, 64))
                out[c, 2 * i + 1, rows, :] = jnp.where(low, roll(left, 64), right)


def shape(*dims):
    return jax.ShapeDtypeStruct(dims, jnp.float32)


def params(mib):
    return pltpu.CompilerParams(vmem_limit_bytes=mib << 20)


def right_pairs():
    pairs = []
    for az in range(16):
        for wn in range(8):
            group, core, y, deep = az // 2, az % 2, wn // 2, wn % 2
            strip = 2 * (2 * group + (deep ^ (group % 2))) + core
            strip = (strip + 1) % 32
            group, core = strip // 4, strip % 2
            deep = (strip // 2 % 2) ^ (group % 2)
            pairs.append((az * 8 + wn, (2 * group + core) * 8 + 2 * y + deep))
    return pairs


def local(state, base_flow, az_scale, blow_table, seg_index, porous):
    sector, slab = lax.axis_index("az"), lax.axis_index("wn")
    core, quarter, deep = sector % 2, slab // 2, slab % 2
    flip = (sector // 2 % 2) ^ core
    count = lax.axis_size("az")
    opposite = [(i + count // 2) % count for i in range(count)]

    keep, send, keep_pole, send_pole = pl.pallas_call(
        halves_kernel,
        out_shape=(
            shape(11, 96, 128),
            shape(11, 96, 128),
            shape(11, REACH, 128),
            shape(11, REACH, 128),
        ),
        in_specs=[SMEM, SMEM, VMEM, VMEM, VMEM],
        out_specs=(VMEM,) * 4,
        compiler_params=params(24),
        name="halves",
    )(core[None].astype(jnp.int32), blow_table, state.reshape(20, 96, 128), seg_index, porous)
    swap = [(i, i ^ 1) for i in range(count)]
    keep_pole = lax.ppermute(keep_pole, "az", list(enumerate(opposite)))
    got_pole = lax.ppermute(send_pole, "az", [(i, j ^ 1) for i, j in enumerate(opposite)])
    got = lax.ppermute(send, "az", swap)

    def cycles(x, sign):
        return jnp.concatenate(
            [sign * x[..., REACH - 1 :: -1], x, jnp.zeros_like(x[..., :REACH])], -1
        )

    flow = jnp.concatenate([cycles(base_flow[0], 1.0), cycles(base_flow[1], -1.0)], 0)
    flow = jnp.stack([flow[:, OWN_T * q : OWN_T * q + ROWS] for q in range(4)])
    flow = jnp.pad(0.5 * flow, ((0, 0), (0, 0), (0, 128 - ROWS)))
    near_axis = lax.dynamic_slice_in_dim(cycles(az_scale, -1.0), OWN_T * quarter, ROWS)
    metric = jnp.broadcast_to(near_axis[:, None], (ROWS, 128))
    cycle = lax.broadcasted_iota(jnp.int32, (ROWS, 128), 0) + (OWN_T * quarter - REACH)
    valid = jnp.where(cycle < 96, 1.0, 0.0).astype(jnp.float32)

    pieces, wall = pl.pallas_call(
        windows_kernel,
        out_shape=(shape(8, FLOW + 8, 128), shape(ROWS, 128)),
        in_specs=[SMEM] + [VMEM] * 5,
        out_specs=(VMEM, VMEM),
        compiler_params=params(24),
        name="windows",
    )(
        jnp.stack([quarter, deep, flip]).astype(jnp.int32),
        keep,
        got,
        keep_pole,
        got_pole,
        flow,
    )
    got = lax.all_to_all(pieces, "wn", 0, 0, tiled=True)
    head, tail = pl.pallas_call(
        edges_kernel,
        out_shape=(shape(41, ROWS, 128), shape(41, ROWS, 128)),
        in_specs=[VMEM, VMEM],
        out_specs=(VMEM, VMEM),
        compiler_params=params(24),
        name="edges",
    )(got, wall)
    pairs = right_pairs()
    head = lax.ppermute(head, ("az", "wn"), [(j, i) for i, j in pairs])
    tail = lax.ppermute(tail, ("az", "wn"), pairs)
    speed = got[:, FLOW:, :ROWS].reshape(8, 2, 4, ROWS).transpose(1, 0, 2, 3)
    speed = jnp.broadcast_to(speed.reshape(2, 32, ROWS, 1), (2, 32, ROWS, 128))

    done = pl.pallas_call(
        steps_kernel,
        out_shape=shape(8, 10, OWN_T, 128),
        in_specs=[VMEM] * 7,
        out_specs=VMEM,
        scratch_shapes=[
            pltpu.VMEM((160, ROWS, 128), jnp.float32),
            pltpu.VMEM((2, ROWS, 128), jnp.float32),
        ]
        + [pltpu.VMEM((160, ROWS, 128), jnp.float32)] * 3,
        compiler_params=params(48),
        name="steps",
    )(got, head, tail, speed, metric, valid, wall)
    back = lax.all_to_all(done, "wn", 0, 0, tiled=True)
    other = lax.dynamic_index_in_dim(
        back.reshape(4, 2, 10, OWN_T, 128), 1 - flip, axis=1, keepdims=False
    )
    other = lax.ppermute(other, "az", swap)
    return pl.pallas_call(
        join_kernel,
        out_shape=shape(5, 4, 96, 128),
        in_specs=[SMEM, VMEM, VMEM],
        out_specs=VMEM,
        compiler_params=params(24),
        name="join",
    )(jnp.stack([flip, core]).astype(jnp.int32), back, other)


def solution(mesh):
    return jax.shard_map(
        local,
        mesh=mesh,
        in_specs=(
            P(None, "wn", None, "az"),
            P(None, "wn", None),
            P(),
            P(),
            P(None, "az"),
            P(None, "az"),
        ),
        out_specs=P(None, "wn", None, "az"),
        check_vma=False,
    )
```

```python
import jax
import jax.numpy as jnp
from jax import lax
from jax.experimental import pallas as pl
from jax.experimental.pallas import tpu as pltpu
from jax.sharding import PartitionSpec as P

STEPS = 3
time_step = 0.25
viscosity = 0.05
heat_ratio = 1.4
admittance = 0.6

REACH = 12
OWN_T = 24
ROWS = OWN_T + 2 * REACH
SIDE = 32
FLOW = 10 * ROWS
SIGNS = (1.0, 1.0, -1.0, -1.0, 1.0)
VMEM = pl.BlockSpec(memory_space=pltpu.VMEM)
HBM = pl.BlockSpec(memory_space=pltpu.HBM)
SMEM = pl.BlockSpec(memory_space=pltpu.SMEM)


def lane_of(shape):
    return lax.broadcasted_iota(jnp.int32, shape, len(shape) - 1)


def roll(x, shift):
    shift = shift % 128
    return pltpu.roll(x, shift, x.ndim - 1) if shift else x


def low_lanes(shape):
    return lane_of(shape) < 64


def inner_lanes(shape):
    return lane_of(shape) % 64 < SIDE


def halves_kernel(
    core,
    table,
    state_far,
    seg_far,
    porous_far,
    keep,
    send,
    keep_pole,
    send_pole,
    state,
    seg,
    porous,
    sems,
):
    fetches = [
        pltpu.make_async_copy(state_far, state, sems.at[0]),
        pltpu.make_async_copy(seg_far, seg, sems.at[1]),
        pltpu.make_async_copy(porous_far, porous, sems.at[2]),
    ]
    for fetch in fetches:
        fetch.start()
    for fetch in fetches:
        fetch.wait()
    first = core[0] == 0
    low = low_lanes((96, 128))

    def split(tile, even, odd, sign):
        left = jnp.where(low, even, roll(odd, 64))
        right = jnp.where(low, roll(even, 64), odd)
        keep[tile] = jnp.where(first, left, right)
        send[tile] = jnp.where(first, right, left)
        for i in range(REACH):
            keep_pole[tile, pl.ds(REACH - 1 - i, 1), :] = sign * keep[tile, pl.ds(i, 1), :]
            send_pole[tile, pl.ds(REACH - 1 - i, 1), :] = sign * send[tile, pl.ds(i, 1), :]

    for c in range(5):
        for i in range(2):
            split(c * 2 + i, state[c * 4 + 2 * i], state[c * 4 + 2 * i + 1], SIGNS[c])
    seg_now = seg[...]
    blowing = jnp.zeros(seg_now.shape, jnp.float32)
    for k in range(16):
        blowing = jnp.where(seg_now == k, table[k], blowing)
    split(10, 2.0 * blowing, porous[...].astype(jnp.float32), 1.0)


def windows_kernel(place, keep, got, keep_pole, got_pole, flow, pieces, wall):
    quarter, odd, flip = place[0], place[1], place[2]

    def window(block, pole, tile, q):
        if q == 0:
            return jnp.concatenate([pole[tile], block[tile, 0:36, :]], 0)
        if q == 3:
            return jnp.concatenate([block[tile, 60:96, :], jnp.zeros((12, 128), jnp.float32)], 0)
        return block[tile, 24 * q - 12 : 24 * q + 36, :]

    for block, pole, spot in ((keep, keep_pole, flip), (got, got_pole, 1 - flip)):
        for q in range(4):
            for tile in range(10):
                pieces[4 * (q // 2) + 2 * spot + q % 2, tile * ROWS : (tile + 1) * ROWS, :] = window(
                    block, pole, tile, q
                )
            pieces[4 * (q // 2) + 2 * spot + q % 2, FLOW : FLOW + 8, :] = flow[q]

            @pl.when(jnp.logical_and(quarter == q, odd == spot))
            def _():
                wall[...] = window(block, pole, 10, q)


def edges_kernel(got, wall, head, tail):
    inner = inner_lanes((ROWS, 128))

    def pack(w, _):
        for c in range(1, 5):
            one = got[w, 2 * c * ROWS : (2 * c + 1) * ROWS, :]
            two = got[w, (2 * c + 1) * ROWS : (2 * c + 2) * ROWS, :]
            turned = roll(one, 64)
            head[w * 4 + c - 1] = jnp.where(inner, turned, roll(two, 64 + SIDE))
            tail[w * 4 + c - 1] = jnp.where(inner, roll(two, 64 - SIDE), turned)
        return 0

    lax.fori_loop(0, 8, pack, 0)
    turned = roll(wall[...], 64)
    head[32] = turned
    tail[32] = turned


def steps_kernel(
    got_far,
    head_far,
    tail_far,
    speed_far,
    metric,
    valid,
    packed_wall,
    out,
    got,
    head,
    tail,
    speed,
    start,
    wall,
    buf_b,
    buf_c,
    buf_d,
    sems,
):
    nu = viscosity
    lane = lane_of((8, 128))

    low = low_lanes((ROWS, 128))
    inner = inner_lanes((ROWS, 128))

    def widen(own, sides):
        return jnp.where(low, own, sides), roll(jnp.where(low, sides, own), 64)

    def fetches(w):
        part = pl.ds(w * 4, 4)
        return (
            pltpu.make_async_copy(got_far.at[w], got.at[w], sems.at[w, 0]),
            pltpu.make_async_copy(head_far.at[part], head.at[part], sems.at[w, 1]),
            pltpu.make_async_copy(tail_far.at[part], tail.at[part], sems.at[w, 2]),
        )

    ends = (
        pltpu.make_async_copy(head_far.at[32], head.at[32], sems.at[8, 0]),
        pltpu.make_async_copy(tail_far.at[32], tail.at[32], sems.at[8, 1]),
        pltpu.make_async_copy(speed_far, speed, sems.at[8, 2]),
    )
    for w in range(8):
        for fetch in fetches(w):
            fetch.start()
    for fetch in ends:
        fetch.start()

    def spread(w, _):
        for fetch in fetches(w):
            fetch.wait()
        for c in range(5):
            one = got[w, 2 * c * ROWS : (2 * c + 1) * ROWS, :]
            two = got[w, (2 * c + 1) * ROWS : (2 * c + 2) * ROWS, :]
            if c:
                right, left = head[w * 4 + c - 1], tail[w * 4 + c - 1]
                pair = widen(one, jnp.where(inner, right, left))
                pair += widen(two, jnp.where(inner, roll(right, -SIDE), roll(left, SIDE)))
            else:
                pair = (one, roll(one, 64), two, roll(two, 64))
            for l in range(4):
                start[w * 20 + c * 4 + l] = pair[l]
        return 0

    lax.fori_loop(0, 8, spread, 0)
    for fetch in ends:
        fetch.wait()
    wall[0], wall[1] = widen(packed_wall[...], jnp.where(inner, head[32], tail[32]))

    def stage_pass(source, base, target, scale, stage, last):
        low, high = stage, ROWS - stage

        def chunk(i, _):
            t0 = jnp.minimum(low + 8 * i, high - 8)
            here = pl.ds(t0, 8)
            m = metric[here, :]
            cm = scale * valid[here, :]
            ch = 0.5 * cm
            c_nu = nu * cm
            ca = (0.25 * c_nu) * (m * m)
            cc = -(4.0 * c_nu + 2.0 * ca)
            cmm = ch * m
            blow = wall[0, here, :]
            coated = wall[1, here, :] > 0.5

            def read(ref, w, c, l, rows=here):
                return ref[w * 20 + c * 4 + l, rows, :]

            def advance(w, carry):
                before, now = carry
                saved = []
                for l in range(4):
                    r = w * 4 + l + 1
                    if r < 32:
                        after = [read(source, r // 4, c, r % 4) for c in range(5)]
                    else:
                        after = [jnp.zeros((8, 128), jnp.float32)] * 5
                    down = [read(source, w, c, l, pl.ds(t0 - 1, 8)) for c in range(5)]
                    up = [read(source, w, c, l, pl.ds(t0 + 1, 8)) for c in range(5)]
                    hu = cm * speed[0, w * 4 + l, here, :]
                    hv = cm * speed[1, w * 4 + l, here, :]
                    rp, rm, tp, tm = c_nu - hu, c_nu + hu, c_nu - hv, c_nu + hv
                    dr_p = after[4] - before[4]
                    dt_p = up[4] - down[4]
                    da_p = roll(now[4], -1) - roll(now[4], 1)
                    div = (after[1] - before[1]) + (up[2] - down[2])
                    div = div + m * (roll(now[3], -1) - roll(now[3], 1))
                    div = ch * div
                    adv = hu * (after[0] - before[0]) + hv * (up[0] - down[0])
                    adv_p = hu * dr_p + hv * dt_p
                    old = [read(base, w, c, l) for c in range(5)]
                    new = [old[0] - adv - div, None, None, None, old[4] - adv_p - heat_ratio * div]
                    push = [None, ch * dr_p, ch * dt_p, cmm * da_p]
                    for c in (1, 2, 3):
                        v = rp * after[c] + rm * before[c] + tp * up[c] + tm * down[c]
                        v = v + ca * (roll(now[c], 2) + roll(now[c], -2)) + cc * now[c]
                        new[c] = old[c] + (v - push[c])
                    if not last:
                        for c in range(5):
                            target[w * 20 + c * 4 + l, here, :] = new[c]
                    elif l % 2 == 0:
                        saved = new
                    else:
                        for c in range(5):
                            both = jnp.where(
                                lane < 64, saved[c], roll(new[c], 64)
                            )
                            out[w, c * 2 + l // 2, pl.ds(t0 - REACH, 8), :] = both
                    before, now = now, after
                return before, now

            first = [read(source, 0, c, 0) for c in range(5)]
            ghost_u = jnp.where(coated, (2.0 * admittance) * first[4], blow) - first[1]
            ghost = [first[0], ghost_u, -first[2], -first[3], first[4]]
            carry = (ghost, first)
            for w in range(8):
                carry = advance(w, carry)
            return 0

        lax.fori_loop(0, (high - low + 7) // 8, chunk, 0, unroll=2)

    h = time_step
    bases = [start, buf_d, start]
    stage = 0
    for step in range(STEPS):
        base = start if step == 0 else buf_d
        plan = [
            (base, buf_b, h / 4.0),
            (buf_b, buf_c, h / 3.0),
            (buf_c, buf_b, h / 2.0),
            (buf_b, buf_d, h),
        ]
        if step == 1:
            plan[3] = (buf_b, buf_c, h)
        if step == 2:
            base = buf_c
            plan = [
                (buf_c, buf_b, h / 4.0),
                (buf_b, buf_d, h / 3.0),
                (buf_d, buf_b, h / 2.0),
                (buf_b, None, h),
            ]
        for source, target, scale in plan:
            stage += 1
            stage_pass(source, base, target, scale, stage, stage == 4 * STEPS)


def join_kernel(place, back, got, out):
    flip, first = place[0], place[1] == 0
    low = low_lanes((OWN_T, 128))
    for q in range(4):
        rows = pl.ds(OWN_T * q, OWN_T)
        for c in range(5):
            for i in range(2):
                mine, other = back[4 * (q // 2) + 2 * flip + q % 2, c * 2 + i], got[q, c * 2 + i]
                left = jnp.where(first, mine, other)
                right = jnp.where(first, other, mine)
                out[c, 2 * i, rows, :] = jnp.where(low, left, roll(right, 64))
                out[c, 2 * i + 1, rows, :] = jnp.where(low, roll(left, 64), right)


def shape(*dims):
    return jax.ShapeDtypeStruct(dims, jnp.float32)


def params(mib):
    return pltpu.CompilerParams(vmem_limit_bytes=mib << 20)


def right_pairs():
    pairs = []
    for az in range(16):
        for wn in range(8):
            group, core, odd = az // 2, az % 2, wn // 2 % 2
            strip = 2 * (2 * group + (odd ^ (group % 2))) + core
            strip = (strip + 1) % 32
            group, core = strip // 4, strip % 2
            other = wn + 2 * (((strip // 2 % 2) ^ (group % 2)) - odd)
            pairs.append((az * 8 + wn, (2 * group + core) * 8 + other))
    return pairs


def local(state, base_flow, az_scale, blow_table, seg_index, porous):
    sector, slab = lax.axis_index("az"), lax.axis_index("wn")
    core, quarter, odd = sector % 2, slab // 4 * 2 + slab % 2, slab // 2 % 2
    flip = (sector // 2 % 2) ^ core
    count = lax.axis_size("az")
    opposite = [(i + count // 2) % count for i in range(count)]

    keep, send, keep_pole, send_pole = pl.pallas_call(
        halves_kernel,
        out_shape=(
            shape(11, 96, 128),
            shape(11, 96, 128),
            shape(11, REACH, 128),
            shape(11, REACH, 128),
        ),
        in_specs=[SMEM, SMEM, HBM, HBM, HBM],
        out_specs=(VMEM,) * 4,
        scratch_shapes=[
            pltpu.VMEM((20, 96, 128), jnp.float32),
            pltpu.VMEM((96, 128), jnp.int32),
            pltpu.VMEM((96, 128), jnp.int32),
            pltpu.SemaphoreType.DMA((3,)),
        ],
        compiler_params=params(24),
        name="halves",
    )(core[None].astype(jnp.int32), blow_table, state.reshape(20, 96, 128), seg_index, porous)
    swap = [(i, i ^ 1) for i in range(count)]
    keep_pole = lax.ppermute(keep_pole, "az", list(enumerate(opposite)))
    got_pole = lax.ppermute(send_pole, "az", [(i, j ^ 1) for i, j in enumerate(opposite)])
    got = lax.ppermute(send, "az", swap)

    def cycles(x, sign):
        return jnp.concatenate(
            [sign * x[..., REACH - 1 :: -1], x, jnp.zeros_like(x[..., :REACH])], -1
        )

    flow = jnp.concatenate([cycles(base_flow[0], 1.0), cycles(base_flow[1], -1.0)], 0)
    flow = jnp.stack([flow[:, OWN_T * q : OWN_T * q + ROWS] for q in range(4)])
    flow = jnp.pad(0.5 * flow, ((0, 0), (0, 0), (0, 128 - ROWS)))
    near_axis = lax.dynamic_slice_in_dim(cycles(az_scale, -1.0), OWN_T * quarter, ROWS)
    metric = jnp.broadcast_to(near_axis[:, None], (ROWS, 128))
    cycle = lax.broadcasted_iota(jnp.int32, (ROWS, 128), 0) + (OWN_T * quarter - REACH)
    valid = jnp.where(cycle < 96, 1.0, 0.0).astype(jnp.float32)

    pieces, wall = pl.pallas_call(
        windows_kernel,
        out_shape=(shape(8, FLOW + 8, 128), shape(ROWS, 128)),
        in_specs=[SMEM] + [VMEM] * 5,
        out_specs=(VMEM, VMEM),
        compiler_params=params(24),
        name="windows",
    )(
        jnp.stack([quarter, odd, flip]).astype(jnp.int32),
        keep,
        got,
        keep_pole,
        got_pole,
        flow,
    )
    got = lax.all_to_all(pieces, "wn", 0, 0, tiled=True)
    head, tail = pl.pallas_call(
        edges_kernel,
        out_shape=(shape(33, ROWS, 128), shape(33, ROWS, 128)),
        in_specs=[VMEM, VMEM],
        out_specs=(VMEM, VMEM),
        compiler_params=params(24),
        name="edges",
    )(got, wall)
    pairs = right_pairs()
    head = lax.ppermute(head, ("az", "wn"), [(j, i) for i, j in pairs])
    tail = lax.ppermute(tail, ("az", "wn"), pairs)
    speed = got[:, FLOW:, :ROWS].reshape(8, 2, 4, ROWS).transpose(1, 0, 2, 3)
    speed = jnp.broadcast_to(speed.reshape(2, 32, ROWS, 1), (2, 32, ROWS, 128))

    done = pl.pallas_call(
        steps_kernel,
        out_shape=shape(8, 10, OWN_T, 128),
        in_specs=[HBM] * 4 + [VMEM] * 3,
        out_specs=VMEM,
        scratch_shapes=[
            pltpu.VMEM((8, FLOW + 8, 128), jnp.float32),
            pltpu.VMEM((33, ROWS, 128), jnp.float32),
            pltpu.VMEM((33, ROWS, 128), jnp.float32),
            pltpu.VMEM((2, 32, ROWS, 128), jnp.float32),
            pltpu.VMEM((160, ROWS, 128), jnp.float32),
            pltpu.VMEM((2, ROWS, 128), jnp.float32),
        ]
        + [pltpu.VMEM((160, ROWS, 128), jnp.float32)] * 3
        + [pltpu.SemaphoreType.DMA((9, 3))],
        compiler_params=params(48),
        name="steps",
    )(got, head, tail, speed, metric, valid, wall)
    back = lax.all_to_all(done, "wn", 0, 0, tiled=True)
    other = lax.dynamic_index_in_dim(
        back.reshape(2, 2, 2, 10, OWN_T, 128), 1 - flip, axis=1, keepdims=False
    ).reshape(4, 10, OWN_T, 128)
    other = lax.ppermute(other, "az", swap)
    return pl.pallas_call(
        join_kernel,
        out_shape=shape(5, 4, 96, 128),
        in_specs=[SMEM, VMEM, VMEM],
        out_specs=VMEM,
        compiler_params=params(24),
        name="join",
    )(jnp.stack([flip, core]).astype(jnp.int32), back, other)


def solution(mesh):
    return jax.shard_map(
        local,
        mesh=mesh,
        in_specs=(
            P(None, "wn", None, "az"),
            P(None, "wn", None),
            P(),
            P(),
            P(None, "az"),
            P(None, "az"),
        ),
        out_specs=P(None, "wn", None, "az"),
        check_vma=False,
    )
```

```python
import jax
import jax.numpy as jnp
from jax import lax
from jax.experimental import pallas as pl
from jax.experimental.pallas import tpu as pltpu
from jax.sharding import PartitionSpec as P

STEPS = 3
time_step = 0.25
viscosity = 0.05
heat_ratio = 1.4
admittance = 0.6

REACH = 12
OWN_T = 24
ROWS = OWN_T + 2 * REACH
SIDE = 32
FLOW = 10 * ROWS
SIGNS = (1.0, 1.0, -1.0, -1.0, 1.0)
VMEM = pl.BlockSpec(memory_space=pltpu.VMEM)
HBM = pl.BlockSpec(memory_space=pltpu.HBM)
SMEM = pl.BlockSpec(memory_space=pltpu.SMEM)


def lane_of(shape):
    return lax.broadcasted_iota(jnp.int32, shape, len(shape) - 1)


def roll(x, shift):
    shift = shift % 128
    return pltpu.roll(x, shift, x.ndim - 1) if shift else x


def low_lanes(shape):
    return lane_of(shape) < 64


def inner_lanes(shape):
    return lane_of(shape) % 64 < SIDE


def halves_kernel(
    core,
    table,
    state_far,
    seg_far,
    porous_far,
    keep,
    send,
    keep_pole,
    send_pole,
    state,
    seg,
    porous,
    sems,
):
    fetches = [
        pltpu.make_async_copy(state_far, state, sems.at[0]),
        pltpu.make_async_copy(seg_far, seg, sems.at[1]),
        pltpu.make_async_copy(porous_far, porous, sems.at[2]),
    ]
    for fetch in fetches:
        fetch.start()
    for fetch in fetches:
        fetch.wait()
    first = core[0] == 0
    low = low_lanes((96, 128))

    def split(tile, even, odd, sign):
        left = jnp.where(low, even, roll(odd, 64))
        right = jnp.where(low, roll(even, 64), odd)
        keep[tile] = jnp.where(first, left, right)
        send[tile] = jnp.where(first, right, left)
        for i in range(REACH):
            keep_pole[tile, pl.ds(REACH - 1 - i, 1), :] = sign * keep[tile, pl.ds(i, 1), :]
            send_pole[tile, pl.ds(REACH - 1 - i, 1), :] = sign * send[tile, pl.ds(i, 1), :]

    for c in range(5):
        for i in range(2):
            split(c * 2 + i, state[c * 4 + 2 * i], state[c * 4 + 2 * i + 1], SIGNS[c])
    seg_now = seg[...]
    blowing = jnp.zeros(seg_now.shape, jnp.float32)
    for k in range(16):
        blowing = jnp.where(seg_now == k, table[k], blowing)
    split(10, 2.0 * blowing, porous[...].astype(jnp.float32), 1.0)


def windows_kernel(place, keep, got, keep_pole, got_pole, flow, pieces, wall):
    quarter, odd, flip = place[0], place[1], place[2]

    def window(block, pole, tile, q):
        if q == 0:
            return jnp.concatenate([pole[tile], block[tile, 0:36, :]], 0)
        if q == 3:
            return jnp.concatenate([block[tile, 60:96, :], jnp.zeros((12, 128), jnp.float32)], 0)
        return block[tile, 24 * q - 12 : 24 * q + 36, :]

    for block, pole, spot in ((keep, keep_pole, flip), (got, got_pole, 1 - flip)):
        for q in range(4):
            for tile in range(10):
                pieces[4 * (q // 2) + 2 * spot + q % 2, tile * ROWS : (tile + 1) * ROWS, :] = window(
                    block, pole, tile, q
                )
            pieces[4 * (q // 2) + 2 * spot + q % 2, FLOW : FLOW + 8, :] = flow[q]

            @pl.when(jnp.logical_and(quarter == q, odd == spot))
            def _():
                wall[...] = window(block, pole, 10, q)


def edges_kernel(got, wall, head, tail):
    inner = inner_lanes((ROWS, 128))

    def pack(w, _):
        for c in range(1, 5):
            one = got[w, 2 * c * ROWS : (2 * c + 1) * ROWS, :]
            two = got[w, (2 * c + 1) * ROWS : (2 * c + 2) * ROWS, :]
            turned = roll(one, 64)
            head[w * 4 + c - 1] = jnp.where(inner, turned, roll(two, 64 + SIDE))
            tail[w * 4 + c - 1] = jnp.where(inner, roll(two, 64 - SIDE), turned)
        return 0

    lax.fori_loop(0, 8, pack, 0, unroll=2)
    turned = roll(wall[...], 64)
    head[32] = turned
    tail[32] = turned


def steps_kernel(
    got_far,
    head_far,
    tail_far,
    speed_far,
    metric,
    valid,
    packed_wall,
    out,
    got,
    head,
    tail,
    speed,
    start,
    wall,
    buf_b,
    buf_c,
    buf_d,
    sems,
):
    nu = viscosity
    lane = lane_of((8, 128))

    low = low_lanes((ROWS, 128))
    inner = inner_lanes((ROWS, 128))

    def widen(own, sides):
        return jnp.where(low, own, sides), roll(jnp.where(low, sides, own), 64)

    def fetches(w):
        part = pl.ds(w * 4, 4)
        return (
            pltpu.make_async_copy(got_far.at[w], got.at[w], sems.at[w, 0]),
            pltpu.make_async_copy(head_far.at[part], head.at[part], sems.at[w, 1]),
            pltpu.make_async_copy(tail_far.at[part], tail.at[part], sems.at[w, 2]),
        )

    ends = (
        pltpu.make_async_copy(head_far.at[32], head.at[32], sems.at[8, 0]),
        pltpu.make_async_copy(tail_far.at[32], tail.at[32], sems.at[8, 1]),
        pltpu.make_async_copy(speed_far, speed, sems.at[8, 2]),
    )
    for w in range(8):
        for fetch in fetches(w):
            fetch.start()
    for fetch in ends:
        fetch.start()

    def spread(w, _):
        for fetch in fetches(w):
            fetch.wait()
        for c in range(5):
            one = got[w, 2 * c * ROWS : (2 * c + 1) * ROWS, :]
            two = got[w, (2 * c + 1) * ROWS : (2 * c + 2) * ROWS, :]
            if c:
                right, left = head[w * 4 + c - 1], tail[w * 4 + c - 1]
                pair = widen(one, jnp.where(inner, right, left))
                pair += widen(two, jnp.where(inner, roll(right, -SIDE), roll(left, SIDE)))
            else:
                pair = (one, roll(one, 64), two, roll(two, 64))
            for l in range(4):
                start[w * 20 + c * 4 + l] = pair[l]
        return 0

    lax.fori_loop(0, 8, spread, 0, unroll=2)
    for fetch in ends:
        fetch.wait()
    wall[0], wall[1] = widen(packed_wall[...], jnp.where(inner, head[32], tail[32]))

    def stage_pass(source, base, target, scale, stage, last):
        low, high = stage, ROWS - stage

        def chunk(i, _):
            t0 = jnp.minimum(low + 8 * i, high - 8)
            here = pl.ds(t0, 8)
            m = metric[here, :]
            cm = scale * valid[here, :]
            ch = 0.5 * cm
            c_nu = nu * cm
            ca = (0.25 * c_nu) * (m * m)
            cc = -(4.0 * c_nu + 2.0 * ca)
            cmm = ch * m
            blow = wall[0, here, :]
            coated = wall[1, here, :] > 0.5

            def read(ref, w, c, l, rows=here):
                return ref[w * 20 + c * 4 + l, rows, :]

            def advance(w, carry):
                before, now = carry
                saved = []
                for l in range(4):
                    r = w * 4 + l + 1
                    if r < 32:
                        after = [read(source, r // 4, c, r % 4) for c in range(5)]
                    else:
                        after = [jnp.zeros((8, 128), jnp.float32)] * 5
                    down = [read(source, w, c, l, pl.ds(t0 - 1, 8)) for c in range(5)]
                    up = [read(source, w, c, l, pl.ds(t0 + 1, 8)) for c in range(5)]
                    hu = cm * speed[0, w * 4 + l, here, :]
                    hv = cm * speed[1, w * 4 + l, here, :]
                    rp, rm, tp, tm = c_nu - hu, c_nu + hu, c_nu - hv, c_nu + hv
                    dr_p = after[4] - before[4]
                    dt_p = up[4] - down[4]
                    da_p = roll(now[4], -1) - roll(now[4], 1)
                    div = (after[1] - before[1]) + (up[2] - down[2])
                    div = div + m * (roll(now[3], -1) - roll(now[3], 1))
                    div = ch * div
                    adv = hu * (after[0] - before[0]) + hv * (up[0] - down[0])
                    adv_p = hu * dr_p + hv * dt_p
                    old = [read(base, w, c, l) for c in range(5)]
                    new = [old[0] - adv - div, None, None, None, old[4] - adv_p - heat_ratio * div]
                    push = [None, ch * dr_p, ch * dt_p, cmm * da_p]
                    for c in (1, 2, 3):
                        v = rp * after[c] + rm * before[c] + tp * up[c] + tm * down[c]
                        v = v + ca * (roll(now[c], 2) + roll(now[c], -2)) + cc * now[c]
                        new[c] = old[c] + (v - push[c])
                    if not last:
                        for c in range(5):
                            target[w * 20 + c * 4 + l, here, :] = new[c]
                    elif l % 2 == 0:
                        saved = new
                    else:
                        for c in range(5):
                            both = jnp.where(
                                lane < 64, saved[c], roll(new[c], 64)
                            )
                            out[w, c * 2 + l // 2, pl.ds(t0 - REACH, 8), :] = both
                    before, now = now, after
                return before, now

            first = [read(source, 0, c, 0) for c in range(5)]
            ghost_u = jnp.where(coated, (2.0 * admittance) * first[4], blow) - first[1]
            ghost = [first[0], ghost_u, -first[2], -first[3], first[4]]
            carry = (ghost, first)
            for w in range(8):
                carry = advance(w, carry)
            return 0

        lax.fori_loop(0, (high - low + 7) // 8, chunk, 0, unroll=3)

    h = time_step
    bases = [start, buf_d, start]
    stage = 0
    for step in range(STEPS):
        base = start if step == 0 else buf_d
        plan = [
            (base, buf_b, h / 4.0),
            (buf_b, buf_c, h / 3.0),
            (buf_c, buf_b, h / 2.0),
            (buf_b, buf_d, h),
        ]
        if step == 1:
            plan[3] = (buf_b, buf_c, h)
        if step == 2:
            base = buf_c
            plan = [
                (buf_c, buf_b, h / 4.0),
                (buf_b, buf_d, h / 3.0),
                (buf_d, buf_b, h / 2.0),
                (buf_b, None, h),
            ]
        for source, target, scale in plan:
            stage += 1
            stage_pass(source, base, target, scale, stage, stage == 4 * STEPS)


def join_kernel(place, back, got, out):
    flip, first = place[0], place[1] == 0
    low = low_lanes((OWN_T, 128))
    for q in range(4):
        rows = pl.ds(OWN_T * q, OWN_T)
        for c in range(5):
            for i in range(2):
                mine, other = back[4 * (q // 2) + 2 * flip + q % 2, c * 2 + i], got[q, c * 2 + i]
                left = jnp.where(first, mine, other)
                right = jnp.where(first, other, mine)
                out[c, 2 * i, rows, :] = jnp.where(low, left, roll(right, 64))
                out[c, 2 * i + 1, rows, :] = jnp.where(low, roll(left, 64), right)


def shape(*dims):
    return jax.ShapeDtypeStruct(dims, jnp.float32)


def params(mib):
    return pltpu.CompilerParams(vmem_limit_bytes=mib << 20)


def right_pairs():
    pairs = []
    for az in range(16):
        for wn in range(8):
            group, core, odd = az // 2, az % 2, wn // 2 % 2
            strip = 2 * (2 * group + (odd ^ (group % 2))) + core
            strip = (strip + 1) % 32
            group, core = strip // 4, strip % 2
            other = wn + 2 * (((strip // 2 % 2) ^ (group % 2)) - odd)
            pairs.append((az * 8 + wn, (2 * group + core) * 8 + other))
    return pairs


def local(state, base_flow, az_scale, blow_table, seg_index, porous):
    sector, slab = lax.axis_index("az"), lax.axis_index("wn")
    core, quarter, odd = sector % 2, slab // 4 * 2 + slab % 2, slab // 2 % 2
    flip = (sector // 2 % 2) ^ core
    count = lax.axis_size("az")
    opposite = [(i + count // 2) % count for i in range(count)]

    keep, send, keep_pole, send_pole = pl.pallas_call(
        halves_kernel,
        out_shape=(
            shape(11, 96, 128),
            shape(11, 96, 128),
            shape(11, REACH, 128),
            shape(11, REACH, 128),
        ),
        in_specs=[SMEM, SMEM, HBM, HBM, HBM],
        out_specs=(VMEM,) * 4,
        scratch_shapes=[
            pltpu.VMEM((20, 96, 128), jnp.float32),
            pltpu.VMEM((96, 128), jnp.int32),
            pltpu.VMEM((96, 128), jnp.int32),
            pltpu.SemaphoreType.DMA((3,)),
        ],
        compiler_params=params(24),
        name="halves",
    )(core[None].astype(jnp.int32), blow_table, state.reshape(20, 96, 128), seg_index, porous)
    swap = [(i, i ^ 1) for i in range(count)]
    keep_pole = lax.ppermute(keep_pole, "az", list(enumerate(opposite)))
    got_pole = lax.ppermute(send_pole, "az", [(i, j ^ 1) for i, j in enumerate(opposite)])
    got = lax.ppermute(send, "az", swap)

    def cycles(x, sign):
        return jnp.concatenate(
            [sign * x[..., REACH - 1 :: -1], x, jnp.zeros_like(x[..., :REACH])], -1
        )

    flow = jnp.concatenate([cycles(base_flow[0], 1.0), cycles(base_flow[1], -1.0)], 0)
    flow = jnp.stack([flow[:, OWN_T * q : OWN_T * q + ROWS] for q in range(4)])
    flow = jnp.pad(0.5 * flow, ((0, 0), (0, 0), (0, 128 - ROWS)))
    near_axis = lax.dynamic_slice_in_dim(cycles(az_scale, -1.0), OWN_T * quarter, ROWS)
    metric = jnp.broadcast_to(near_axis[:, None], (ROWS, 128))
    cycle = lax.broadcasted_iota(jnp.int32, (ROWS, 128), 0) + (OWN_T * quarter - REACH)
    valid = jnp.where(cycle < 96, 1.0, 0.0).astype(jnp.float32)

    pieces, wall = pl.pallas_call(
        windows_kernel,
        out_shape=(shape(8, FLOW + 8, 128), shape(ROWS, 128)),
        in_specs=[SMEM] + [VMEM] * 5,
        out_specs=(VMEM, VMEM),
        compiler_params=params(24),
        name="windows",
    )(
        jnp.stack([quarter, odd, flip]).astype(jnp.int32),
        keep,
        got,
        keep_pole,
        got_pole,
        flow,
    )
    got = lax.all_to_all(pieces, "wn", 0, 0, tiled=True)
    head, tail = pl.pallas_call(
        edges_kernel,
        out_shape=(shape(33, ROWS, 128), shape(33, ROWS, 128)),
        in_specs=[VMEM, VMEM],
        out_specs=(VMEM, VMEM),
        compiler_params=params(24),
        name="edges",
    )(got, wall)
    pairs = right_pairs()
    head = lax.ppermute(head, ("az", "wn"), [(j, i) for i, j in pairs])
    tail = lax.ppermute(tail, ("az", "wn"), pairs)
    speed = got[:, FLOW:, :ROWS].reshape(8, 2, 4, ROWS).transpose(1, 0, 2, 3)
    speed = jnp.broadcast_to(speed.reshape(2, 32, ROWS, 1), (2, 32, ROWS, 128))

    done = pl.pallas_call(
        steps_kernel,
        out_shape=shape(8, 10, OWN_T, 128),
        in_specs=[HBM] * 4 + [VMEM] * 3,
        out_specs=VMEM,
        scratch_shapes=[
            pltpu.VMEM((8, FLOW + 8, 128), jnp.float32),
            pltpu.VMEM((33, ROWS, 128), jnp.float32),
            pltpu.VMEM((33, ROWS, 128), jnp.float32),
            pltpu.VMEM((2, 32, ROWS, 128), jnp.float32),
            pltpu.VMEM((160, ROWS, 128), jnp.float32),
            pltpu.VMEM((2, ROWS, 128), jnp.float32),
        ]
        + [pltpu.VMEM((160, ROWS, 128), jnp.float32)] * 3
        + [pltpu.SemaphoreType.DMA((9, 3))],
        compiler_params=params(48),
        name="steps",
    )(got, head, tail, speed, metric, valid, wall)
    back = lax.all_to_all(done, "wn", 0, 0, tiled=True)
    other = lax.dynamic_index_in_dim(
        back.reshape(2, 2, 2, 10, OWN_T, 128), 1 - flip, axis=1, keepdims=False
    ).reshape(4, 10, OWN_T, 128)
    other = lax.ppermute(other, "az", swap)
    return pl.pallas_call(
        join_kernel,
        out_shape=shape(5, 4, 96, 128),
        in_specs=[SMEM, VMEM, VMEM],
        out_specs=VMEM,
        compiler_params=params(24),
        name="join",
    )(jnp.stack([flip, core]).astype(jnp.int32), back, other)


def solution(mesh):
    return jax.shard_map(
        local,
        mesh=mesh,
        in_specs=(
            P(None, "wn", None, "az"),
            P(None, "wn", None),
            P(),
            P(),
            P(None, "az"),
            P(None, "az"),
        ),
        out_specs=P(None, "wn", None, "az"),
        check_vma=False,
    )
```

```python
import jax
import jax.numpy as jnp
from jax import lax
from jax.experimental import pallas as pl
from jax.experimental.pallas import tpu as pltpu
from jax.sharding import PartitionSpec as P

STEPS = 3
time_step = 0.25
viscosity = 0.05
heat_ratio = 1.4
admittance = 0.6

REACH = 12
OWN_T = 24
ROWS = OWN_T + 2 * REACH
SIDE = 32
FLOW = 10 * ROWS
SIGNS = (1.0, 1.0, -1.0, -1.0, 1.0)
VMEM = pl.BlockSpec(memory_space=pltpu.VMEM)
HBM = pl.BlockSpec(memory_space=pltpu.HBM)
SMEM = pl.BlockSpec(memory_space=pltpu.SMEM)


def lane_of(shape):
    return lax.broadcasted_iota(jnp.int32, shape, len(shape) - 1)


def roll(x, shift):
    shift = shift % 128
    return pltpu.roll(x, shift, x.ndim - 1) if shift else x


def low_lanes(shape):
    return lane_of(shape) < 64


def inner_lanes(shape):
    return lane_of(shape) % 64 < SIDE


def halves_kernel(
    core,
    table,
    state_far,
    seg_far,
    porous_far,
    keep,
    send,
    keep_pole,
    send_pole,
    state,
    seg,
    porous,
    sems,
):
    fetches = [
        pltpu.make_async_copy(state_far, state, sems.at[0]),
        pltpu.make_async_copy(seg_far, seg, sems.at[1]),
        pltpu.make_async_copy(porous_far, porous, sems.at[2]),
    ]
    for fetch in fetches:
        fetch.start()
    for fetch in fetches:
        fetch.wait()
    first = core[0] == 0
    low = low_lanes((96, 128))

    def split(tile, even, odd, sign):
        left = jnp.where(low, even, roll(odd, 64))
        right = jnp.where(low, roll(even, 64), odd)
        keep[tile] = jnp.where(first, left, right)
        send[tile] = jnp.where(first, right, left)
        for i in range(REACH):
            keep_pole[tile, pl.ds(REACH - 1 - i, 1), :] = sign * keep[tile, pl.ds(i, 1), :]
            send_pole[tile, pl.ds(REACH - 1 - i, 1), :] = sign * send[tile, pl.ds(i, 1), :]

    for c in range(5):
        for i in range(2):
            split(c * 2 + i, state[c * 4 + 2 * i], state[c * 4 + 2 * i + 1], SIGNS[c])
    seg_now = seg[...]
    blowing = jnp.zeros(seg_now.shape, jnp.float32)
    for k in range(16):
        blowing = jnp.where(seg_now == k, table[k], blowing)
    split(10, 2.0 * blowing, porous[...].astype(jnp.float32), 1.0)


def windows_kernel(place, keep, got, keep_pole, got_pole, flow, pieces, wall):
    quarter, odd, flip = place[0], place[1], place[2]

    def window(block, pole, tile, q):
        if q == 0:
            return jnp.concatenate([pole[tile], block[tile, 0:36, :]], 0)
        if q == 3:
            return jnp.concatenate([block[tile, 60:96, :], jnp.zeros((12, 128), jnp.float32)], 0)
        return block[tile, 24 * q - 12 : 24 * q + 36, :]

    for block, pole, spot in ((keep, keep_pole, flip), (got, got_pole, 1 - flip)):
        for q in range(4):
            for tile in range(10):
                pieces[4 * (q // 2) + 2 * spot + q % 2, tile * ROWS : (tile + 1) * ROWS, :] = window(
                    block, pole, tile, q
                )
            pieces[4 * (q // 2) + 2 * spot + q % 2, FLOW : FLOW + 8, :] = flow[q]

            @pl.when(jnp.logical_and(quarter == q, odd == spot))
            def _():
                wall[...] = window(block, pole, 10, q)


def edges_kernel(got, wall, head, tail):
    inner = inner_lanes((ROWS, 128))

    def pack(w, _):
        for c in range(1, 5):
            one = got[w, 2 * c * ROWS : (2 * c + 1) * ROWS, :]
            two = got[w, (2 * c + 1) * ROWS : (2 * c + 2) * ROWS, :]
            turned = roll(one, 64)
            head[w * 4 + c - 1] = jnp.where(inner, turned, roll(two, 64 + SIDE))
            tail[w * 4 + c - 1] = jnp.where(inner, roll(two, 64 - SIDE), turned)
        return 0

    lax.fori_loop(0, 8, pack, 0, unroll=2)
    turned = roll(wall[...], 64)
    head[32] = turned
    tail[32] = turned


def steps_kernel(
    got_far,
    head_far,
    tail_far,
    speed_far,
    metric,
    valid,
    packed_wall,
    out,
    got,
    head,
    tail,
    speed,
    start,
    wall,
    buf_b,
    buf_c,
    buf_d,
    sems,
):
    nu = viscosity
    lane = lane_of((8, 128))

    low = low_lanes((ROWS, 128))
    inner = inner_lanes((ROWS, 128))

    def widen(own, sides):
        return jnp.where(low, own, sides), roll(jnp.where(low, sides, own), 64)

    def fetches(w):
        part = pl.ds(w * 4, 4)
        return (
            pltpu.make_async_copy(got_far.at[w], got.at[w], sems.at[w, 0]),
            pltpu.make_async_copy(head_far.at[part], head.at[part], sems.at[w, 1]),
            pltpu.make_async_copy(tail_far.at[part], tail.at[part], sems.at[w, 2]),
        )

    ends = (
        pltpu.make_async_copy(head_far.at[32], head.at[32], sems.at[8, 0]),
        pltpu.make_async_copy(tail_far.at[32], tail.at[32], sems.at[8, 1]),
        pltpu.make_async_copy(speed_far, speed, sems.at[8, 2]),
    )
    for w in range(8):
        for fetch in fetches(w):
            fetch.start()
    for fetch in ends:
        fetch.start()

    def spread(w, _):
        for fetch in fetches(w):
            fetch.wait()
        for c in range(5):
            one = got[w, 2 * c * ROWS : (2 * c + 1) * ROWS, :]
            two = got[w, (2 * c + 1) * ROWS : (2 * c + 2) * ROWS, :]
            if c:
                right, left = head[w * 4 + c - 1], tail[w * 4 + c - 1]
                pair = widen(one, jnp.where(inner, right, left))
                pair += widen(two, jnp.where(inner, roll(right, -SIDE), roll(left, SIDE)))
            else:
                pair = (one, roll(one, 64), two, roll(two, 64))
            for l in range(4):
                start[w * 20 + c * 4 + l] = pair[l]
        return 0

    lax.fori_loop(0, 8, spread, 0, unroll=2)
    for fetch in ends:
        fetch.wait()
    wall[0], wall[1] = widen(packed_wall[...], jnp.where(inner, head[32], tail[32]))

    def stage_pass(source, base, target, scale, stage, last):
        low, high = stage, ROWS - stage

        def chunk(i, _):
            t0 = jnp.minimum(low + 8 * i, high - 8)
            here = pl.ds(t0, 8)
            m = metric[here, :]
            cm = scale * valid[here, :]
            ch = 0.5 * cm
            c_nu = nu * cm
            ca = (0.25 * c_nu) * (m * m)
            cc = -(4.0 * c_nu + 2.0 * ca)
            cmm = ch * m
            blow = wall[0, here, :]
            coated = wall[1, here, :] > 0.5

            def read(ref, w, c, l, rows=here):
                return ref[w * 20 + c * 4 + l, rows, :]

            def advance(w, carry):
                before, now = carry
                saved = []
                for l in range(4):
                    r = w * 4 + l + 1
                    if r < 32:
                        after = [read(source, r // 4, c, r % 4) for c in range(5)]
                    else:
                        after = [jnp.zeros((8, 128), jnp.float32)] * 5
                    down = [read(source, w, c, l, pl.ds(t0 - 1, 8)) for c in range(5)]
                    up = [read(source, w, c, l, pl.ds(t0 + 1, 8)) for c in range(5)]
                    hu = cm * speed[0, w * 4 + l, here, :]
                    hv = cm * speed[1, w * 4 + l, here, :]
                    rp, rm, tp, tm = c_nu - hu, c_nu + hu, c_nu - hv, c_nu + hv
                    dr_p = after[4] - before[4]
                    dt_p = up[4] - down[4]
                    da_p = roll(now[4], -1) - roll(now[4], 1)
                    div = (after[1] - before[1]) + (up[2] - down[2])
                    div = div + m * (roll(now[3], -1) - roll(now[3], 1))
                    div = ch * div
                    adv = hu * (after[0] - before[0]) + hv * (up[0] - down[0])
                    adv_p = hu * dr_p + hv * dt_p
                    old = now if base is source else [read(base, w, c, l) for c in range(5)]
                    new = [old[0] - adv - div, None, None, None, old[4] - adv_p - heat_ratio * div]
                    push = [None, ch * dr_p, ch * dt_p, cmm * da_p]
                    for c in (1, 2, 3):
                        v = rp * after[c] + rm * before[c] + tp * up[c] + tm * down[c]
                        v = v + ca * (roll(now[c], 2) + roll(now[c], -2)) + cc * now[c]
                        new[c] = old[c] + (v - push[c])
                    if not last:
                        for c in range(5):
                            target[w * 20 + c * 4 + l, here, :] = new[c]
                    elif l % 2 == 0:
                        saved = new
                    else:
                        for c in range(5):
                            both = jnp.where(
                                lane < 64, saved[c], roll(new[c], 64)
                            )
                            out[w, c * 2 + l // 2, pl.ds(t0 - REACH, 8), :] = both
                    before, now = now, after
                return before, now

            first = [read(source, 0, c, 0) for c in range(5)]
            ghost_u = jnp.where(coated, (2.0 * admittance) * first[4], blow) - first[1]
            ghost = [first[0], ghost_u, -first[2], -first[3], first[4]]
            carry = (ghost, first)
            for w in range(8):
                carry = advance(w, carry)
            return 0

        lax.fori_loop(0, (high - low + 7) // 8, chunk, 0, unroll=3)

    h = time_step
    bases = [start, buf_d, start]
    stage = 0
    for step in range(STEPS):
        base = start if step == 0 else buf_d
        plan = [
            (base, buf_b, h / 4.0),
            (buf_b, buf_c, h / 3.0),
            (buf_c, buf_b, h / 2.0),
            (buf_b, buf_d, h),
        ]
        if step == 1:
            plan[3] = (buf_b, buf_c, h)
        if step == 2:
            base = buf_c
            plan = [
                (buf_c, buf_b, h / 4.0),
                (buf_b, buf_d, h / 3.0),
                (buf_d, buf_b, h / 2.0),
                (buf_b, None, h),
            ]
        for source, target, scale in plan:
            stage += 1
            stage_pass(source, base, target, scale, stage, stage == 4 * STEPS)


def join_kernel(place, back, got, out):
    flip, first = place[0], place[1] == 0
    low = low_lanes((OWN_T, 128))
    for q in range(4):
        rows = pl.ds(OWN_T * q, OWN_T)
        for c in range(5):
            for i in range(2):
                mine, other = back[4 * (q // 2) + 2 * flip + q % 2, c * 2 + i], got[q, c * 2 + i]
                left = jnp.where(first, mine, other)
                right = jnp.where(first, other, mine)
                out[c, 2 * i, rows, :] = jnp.where(low, left, roll(right, 64))
                out[c, 2 * i + 1, rows, :] = jnp.where(low, roll(left, 64), right)


def shape(*dims):
    return jax.ShapeDtypeStruct(dims, jnp.float32)


def params(mib):
    return pltpu.CompilerParams(vmem_limit_bytes=mib << 20)


def right_pairs():
    pairs = []
    for az in range(16):
        for wn in range(8):
            group, core, odd = az // 2, az % 2, wn // 2 % 2
            strip = 2 * (2 * group + (odd ^ (group % 2))) + core
            strip = (strip + 1) % 32
            group, core = strip // 4, strip % 2
            other = wn + 2 * (((strip // 2 % 2) ^ (group % 2)) - odd)
            pairs.append((az * 8 + wn, (2 * group + core) * 8 + other))
    return pairs


def local(state, base_flow, az_scale, blow_table, seg_index, porous):
    sector, slab = lax.axis_index("az"), lax.axis_index("wn")
    core, quarter, odd = sector % 2, slab // 4 * 2 + slab % 2, slab // 2 % 2
    flip = (sector // 2 % 2) ^ core
    count = lax.axis_size("az")
    opposite = [(i + count // 2) % count for i in range(count)]

    keep, send, keep_pole, send_pole = pl.pallas_call(
        halves_kernel,
        out_shape=(
            shape(11, 96, 128),
            shape(11, 96, 128),
            shape(11, REACH, 128),
            shape(11, REACH, 128),
        ),
        in_specs=[SMEM, SMEM, HBM, HBM, HBM],
        out_specs=(VMEM,) * 4,
        scratch_shapes=[
            pltpu.VMEM((20, 96, 128), jnp.float32),
            pltpu.VMEM((96, 128), jnp.int32),
            pltpu.VMEM((96, 128), jnp.int32),
            pltpu.SemaphoreType.DMA((3,)),
        ],
        compiler_params=params(52),
        name="halves",
    )(core[None].astype(jnp.int32), blow_table, state.reshape(20, 96, 128), seg_index, porous)
    swap = [(i, i ^ 1) for i in range(count)]
    keep_pole = lax.ppermute(keep_pole, "az", list(enumerate(opposite)))
    got_pole = lax.ppermute(send_pole, "az", [(i, j ^ 1) for i, j in enumerate(opposite)])
    got = lax.ppermute(send, "az", swap)

    def cycles(x, sign):
        return jnp.concatenate(
            [sign * x[..., REACH - 1 :: -1], x, jnp.zeros_like(x[..., :REACH])], -1
        )

    flow = jnp.concatenate([cycles(base_flow[0], 1.0), cycles(base_flow[1], -1.0)], 0)
    flow = jnp.stack([flow[:, OWN_T * q : OWN_T * q + ROWS] for q in range(4)])
    flow = jnp.pad(0.5 * flow, ((0, 0), (0, 0), (0, 128 - ROWS)))
    near_axis = lax.dynamic_slice_in_dim(cycles(az_scale, -1.0), OWN_T * quarter, ROWS)
    metric = jnp.broadcast_to(near_axis[:, None], (ROWS, 128))
    cycle = lax.broadcasted_iota(jnp.int32, (ROWS, 128), 0) + (OWN_T * quarter - REACH)
    valid = jnp.where(cycle < 96, 1.0, 0.0).astype(jnp.float32)

    pieces, wall = pl.pallas_call(
        windows_kernel,
        out_shape=(shape(8, FLOW + 8, 128), shape(ROWS, 128)),
        in_specs=[SMEM] + [VMEM] * 5,
        out_specs=(VMEM, VMEM),
        compiler_params=params(24),
        name="windows",
    )(
        jnp.stack([quarter, odd, flip]).astype(jnp.int32),
        keep,
        got,
        keep_pole,
        got_pole,
        flow,
    )
    got = lax.all_to_all(pieces, "wn", 0, 0, tiled=True)
    head, tail = pl.pallas_call(
        edges_kernel,
        out_shape=(shape(33, ROWS, 128), shape(33, ROWS, 128)),
        in_specs=[VMEM, VMEM],
        out_specs=(VMEM, VMEM),
        compiler_params=params(24),
        name="edges",
    )(got, wall)
    pairs = right_pairs()
    head = lax.ppermute(head, ("az", "wn"), [(j, i) for i, j in pairs])
    tail = lax.ppermute(tail, ("az", "wn"), pairs)
    speed = got[:, FLOW:, :ROWS].reshape(8, 2, 4, ROWS).transpose(1, 0, 2, 3)
    speed = jnp.broadcast_to(speed.reshape(2, 32, ROWS, 1), (2, 32, ROWS, 128))

    done = pl.pallas_call(
        steps_kernel,
        out_shape=shape(8, 10, OWN_T, 128),
        in_specs=[HBM] * 4 + [VMEM] * 3,
        out_specs=VMEM,
        scratch_shapes=[
            pltpu.VMEM((8, FLOW + 8, 128), jnp.float32),
            pltpu.VMEM((33, ROWS, 128), jnp.float32),
            pltpu.VMEM((33, ROWS, 128), jnp.float32),
            pltpu.VMEM((2, 32, ROWS, 128), jnp.float32),
            pltpu.VMEM((160, ROWS, 128), jnp.float32),
            pltpu.VMEM((2, ROWS, 128), jnp.float32),
        ]
        + [pltpu.VMEM((160, ROWS, 128), jnp.float32)] * 3
        + [pltpu.SemaphoreType.DMA((9, 3))],
        compiler_params=params(48),
        name="steps",
    )(got, head, tail, speed, metric, valid, wall)
    back = lax.all_to_all(done, "wn", 0, 0, tiled=True)
    other = lax.dynamic_index_in_dim(
        back.reshape(2, 2, 2, 10, OWN_T, 128), 1 - flip, axis=1, keepdims=False
    ).reshape(4, 10, OWN_T, 128)
    other = lax.ppermute(other, "az", swap)
    return pl.pallas_call(
        join_kernel,
        out_shape=shape(5, 4, 96, 128),
        in_specs=[SMEM, VMEM, VMEM],
        out_specs=VMEM,
        compiler_params=params(24),
        name="join",
    )(jnp.stack([flip, core]).astype(jnp.int32), back, other)


def solution(mesh):
    return jax.shard_map(
        local,
        mesh=mesh,
        in_specs=(
            P(None, "wn", None, "az"),
            P(None, "wn", None),
            P(),
            P(),
            P(None, "az"),
            P(None, "az"),
        ),
        out_specs=P(None, "wn", None, "az"),
        check_vma=False,
    )
```
